32 devices in a mesh: dp: 16 (over z, y, x), pipe: 2 (over core).
Axes of the slice: x: 2, y: 2, z: 4, core: 2. Of those that a mesh axis runs over, the one named last changes fastest.
Arguments:
- enc_tokens: bfloat16 [2, 1536, 2048], P(None, 'dp'), may hold values from -6 to 6
- dec_tokens: bfloat16 [2, 512, 2048], P(None, 'dp'), may hold values from -6 to 6
- enc_segments: int32 [2, 1536], P(None, 'dp'), may hold values from 0 to 3, as said below
- dec_segments: int32 [2, 512], P(None, 'dp'), may hold values from 0 to 3, as said below
- proj_in: bfloat16 [2, 3, 2048, 128], P('pipe'), may hold values from -0.125 to 0.125
- proj_out: bfloat16 [2, 128, 2048], P('pipe'), may hold values from -0.5 to 0.5
- cotangent: bfloat16 [2, 512, 2048], P(None, 'dp'), may hold values from -6 to 6
Outputs:
- grad_in: float32 [2, 3, 2048, 128], P('pipe', None, 'dp')
- grad_out: float32 [2, 128, 2048], P('pipe', None, 'dp')
The draws below stay inside these ranges and needn't reach their ends.
Inputs may be any that keep to these rules, and one draw needn't show every extreme that they name: `enc_segments`: in each microbatch and each aligned block of 96 encoder rows the ids start at 0, never fall, rise by at most one from row to row and end at 3; equal ids are one packed sample. `dec_segments`: decoder row j of a block carries the id of encoder row (j * 96) // 32 of the same block and microbatch, so every decoder token's sample has encoder tokens.
All inputs are finite; a program needn't handle non-finite values.
Results may differ from the reference program's by a relative error of at most 0.012.
Values may be sent and summed in bfloat16 or wider, within the bound.
A program may use at most 64 MiB of HBM per device.

```python
import math
import jax
import jax.numpy as jnp
from jax import lax

D = 2048
HD = 128
MICRO = 2
TE = 96
TD = 32
LAYERS = 2
ENC_ROWS = 1536
DEC_ROWS = 512
N_DP = 16


def segment_table(key):
    breaks = jax.random.randint(key, (MICRO, N_DP, TE), 0, 24) == 0
    breaks = breaks | (jnp.arange(TE) % (TE // 4) == 0)
    return jnp.minimum(jnp.cumsum(breaks.astype(jnp.int32), axis=-1) - 1, 3)


def draw_enc_segments(key, part):
    table = segment_table(key)
    return table.reshape(MICRO, N_DP * TE)


def draw_dec_segments(key, part):
    table = segment_table(key)
    chosen = jnp.arange(TD) * TE // TD
    return table[:, :, chosen].reshape(MICRO, N_DP * TD)


def levels(stream_key, extent, cuts, low, top_value):
    gain, own = 1.0, jax.random.fold_in(stream_key, 6)
    for dim, shards_of in cuts:
        steps = jnp.exp(jax.random.uniform(jax.random.fold_in(own, dim), (shards_of,), jnp.float32, low / len(cuts), top_value / len(cuts)))
        gain = gain * jnp.repeat(steps, extent[dim] // shards_of).reshape([-1 if axis == dim else 1 for axis in range(len(extent))])
    return gain


def scatter_about(rng, extent, width, limit, cuts=(), kind=jnp.bfloat16):
    gain = levels(rng, extent, cuts, -0.22, 0.18) if cuts else 1.0
    values = jax.random.normal(rng, extent, jnp.float32) * width * gain
    return jnp.minimum(jnp.maximum(values, -limit), limit).astype(kind)


def setup_inputs(seed: int = 0) -> dict:
    streams_of = jax.random.split(jax.random.key(seed), 8)
    return {
        "enc_tokens": scatter_about(streams_of[0], (MICRO, ENC_ROWS, D), 1.0, 6.0, ((1, 16),)),
        "dec_tokens": scatter_about(streams_of[1], (MICRO, DEC_ROWS, D), 1.0, 6.0, ((1, 16),)),
        "enc_segments": draw_enc_segments(jax.random.fold_in(streams_of[7], 71), 0),
        "dec_segments": draw_dec_segments(jax.random.fold_in(streams_of[7], 71), 0),
        "proj_in": scatter_about(streams_of[4], (LAYERS, 3, D, HD), D ** -0.5, 0.125, ((0, 2),)),
        "proj_out": scatter_about(streams_of[5], (LAYERS, HD, D), HD ** -0.5, 0.5, ((0, 2),)),
        "cotangent": scatter_about(streams_of[6], (MICRO, DEC_ROWS, D), 1.0, 6.0, ((1, 16),)),
    }


def normalize(values):
    return values * lax.rsqrt(lax.optimization_barrier(jnp.mean(values * values, axis=-1, keepdims=True)) + 1e-06)

def attention(queries, key_rows, value_rows, allowed):
    scores = jnp.dot(queries, key_rows.T, preferred_element_type=jnp.float32) * (1.0 / math.sqrt(queries.shape[-1]))
    scores = jnp.where(allowed, scores, -1e+30)
    row_max = lax.optimization_barrier(jnp.max(scores, axis=-1, keepdims=True))
    expo = jnp.exp(scores - row_max)
    probabilities = (expo / lax.optimization_barrier(jnp.sum(expo, axis=-1, keepdims=True))).astype(jnp.bfloat16)
    return jnp.dot(probabilities, value_rows, preferred_element_type=jnp.float32).astype(jnp.bfloat16)

def section_apply(weights_in, weights_out, buffer, enc_ids, dec_ids, encoder_layer):
    enc_count = enc_ids.shape[0]
    memory = buffer[:enc_count]
    stream = buffer[enc_count:]
    if encoder_layer:
        residual = memory.astype(jnp.float32)
        normalized = normalize(residual).astype(jnp.bfloat16)
        queries = jnp.dot(normalized, weights_in[0], preferred_element_type=jnp.float32).astype(jnp.bfloat16)
        key_rows = jnp.dot(normalized, weights_in[1], preferred_element_type=jnp.float32).astype(jnp.bfloat16)
        value_rows = jnp.dot(normalized, weights_in[2], preferred_element_type=jnp.float32).astype(jnp.bfloat16)
        allowed = enc_ids[:, None] == enc_ids[None, :]
        attended = attention(queries, key_rows, value_rows, allowed)
        updated = (residual + jnp.dot(attended, weights_out, preferred_element_type=jnp.float32)).astype(jnp.bfloat16)
        return jnp.concatenate([updated, stream], axis=0)
    residual = stream.astype(jnp.float32)
    normalized = normalize(residual).astype(jnp.bfloat16)
    source = normalize(memory.astype(jnp.float32)).astype(jnp.bfloat16)
    queries = jnp.dot(normalized, weights_in[0], preferred_element_type=jnp.float32).astype(jnp.bfloat16)
    key_rows = jnp.dot(source, weights_in[1], preferred_element_type=jnp.float32).astype(jnp.bfloat16)
    value_rows = jnp.dot(source, weights_in[2], preferred_element_type=jnp.float32).astype(jnp.bfloat16)
    allowed = dec_ids[:, None] == enc_ids[None, :]
    attended = attention(queries, key_rows, value_rows, allowed)
    updated = (residual + jnp.dot(attended, weights_out, preferred_element_type=jnp.float32)).astype(jnp.bfloat16)
    return jnp.concatenate([memory, updated], axis=0)

def reference(enc_tokens, dec_tokens, enc_segments, dec_segments, proj_in, proj_out, cotangent):
    layer_count = proj_in.shape[0]

    def shaped(array, row_count):
        return array.reshape((MICRO, N_DP, row_count) + array.shape[2:]).swapaxes(0, 1)
    replica_inputs = (shaped(enc_tokens, TE), shaped(dec_tokens, TD), shaped(enc_segments, TE), shaped(dec_segments, TD), shaped(cotangent, TD))
    list_in = [proj_in[layer_index] for layer_index in range(layer_count)]
    list_out = [proj_out[layer_index] for layer_index in range(layer_count)]

    def replica(running, replica_data):
        total_in, total_out = running
        enc_x, dec_x, enc_ids, dec_ids, seed_rows = replica_data
        for micro_index in range(MICRO):

            def forward(weights_list_in, weights_list_out):
                buffer = jnp.concatenate([enc_x[micro_index], dec_x[micro_index]], axis=0)
                for layer_index in range(layer_count):
                    buffer = section_apply(weights_list_in[layer_index], weights_list_out[layer_index], buffer, enc_ids[micro_index], dec_ids[micro_index], layer_index < layer_count // 2)
                return buffer[TE:]
            output, pullback = jax.vjp(forward, list_in, list_out)
            grads_in, grads_out = pullback(seed_rows[micro_index])
            total_in = total_in + jnp.stack([gradient.astype(jnp.float32) for gradient in grads_in])
            total_out = total_out + jnp.stack([gradient.astype(jnp.float32) for gradient in grads_out])
        return ((total_in, total_out), None)
    start = (jnp.zeros(proj_in.shape, jnp.float32), jnp.zeros(proj_out.shape, jnp.float32))
    (total_in, total_out), unused = lax.scan(replica, start, replica_inputs)
    return (total_in, total_out)
```

```python
import functools
import math

import jax
import jax.numpy as jnp
from jax import lax
from jax.experimental import pallas as pl
from jax.experimental.pallas import tpu as pltpu
from jax.sharding import PartitionSpec as P

BF = jnp.bfloat16
F32 = jnp.float32
MESH = pl.DeviceIdType.MESH
TN = (((1,), (1,)), ((), ()))
NT = (((0,), (0,)), ((), ()))


def dot(a, b):
    return jnp.dot(a, b, preferred_element_type=F32)


def dot_t(a, b):
    return lax.dot_general(a, b, TN, preferred_element_type=F32)


def t_dot(a, b):
    return lax.dot_general(a, b, NT, preferred_element_type=F32)


def one_hot(ids, per_micro, micro_count):
    rows = -(-(4 * micro_count) // 16) * 16
    count = ids.shape[1]
    which = lax.broadcasted_iota(jnp.int32, (rows, count), 0)
    micro = lax.broadcasted_iota(jnp.int32, (rows, count), 1) // per_micro
    return jnp.where(which == ids + 4 * micro, 1.0, 0.0).astype(BF)


def softmax_rows(scores, allowed):
    scores = jnp.where(allowed, scores, -1e30)
    expo = jnp.exp(scores - jnp.max(scores, axis=-1, keepdims=True))
    return expo / jnp.sum(expo, axis=-1, keepdims=True)


def rms_rows(src, dst, scale_ref, step=16):
    for row in range(0, src.shape[0], step):
        x = src[row : row + step, :].astype(F32)
        r = lax.rsqrt(jnp.mean(x * x, axis=-1, keepdims=True) + 1e-06)
        dst[row : row + step, :] = (x * r).astype(BF)
        if scale_ref is not None:
            scale_ref[row : row + step, :] = jnp.broadcast_to(r, (step, 128))


def kernel(
    layers, n, micro_count, parts,
    enc, dec, eid, did, w_in, w_out, cot,
    out_in, out_o,
    inbuf, outbuf, gin, gout, hbuf, mbuf, rbuf, rsbuf, qb, kb, vb, ab, pb, dq, dk, dv, total, *rest,
):
    count = len(parts)
    gs = rest[:count]
    recvs = rest[count : 2 * count]
    fs, fr, bs, br, rs_send, rs_recv = rest[2 * count :]
    bits = n.bit_length() - 1
    half = layers // 2
    te, td = enc.shape[0], dec.shape[0]
    width = enc.shape[1]
    hd = w_in.shape[3]
    scale = 1.0 / math.sqrt(hd)
    deep = layers > 2

    p = lax.axis_index("pipe")
    me = lax.axis_index("dp")
    b = [lax.rem(me // (1 << i), 2) for i in range(bits)]
    partner = [me + (1 - 2 * b[i]) * (1 << i) for i in range(bits)]
    up = lax.rem(p + 1, layers)
    down = lax.rem(p + layers - 1, layers)
    not_first = p > 0
    not_last = p < layers - 1
    is_enc = p < half

    barrier = pltpu.get_barrier_semaphore()
    for q in partner:
        pl.semaphore_signal(barrier, inc=1, device_id=(q, p), device_id_type=MESH)

    @pl.when(not_first)
    def _():
        pl.semaphore_signal(barrier, inc=1, device_id=(me, down), device_id_type=MESH)

    @pl.when(not_last)
    def _():
        pl.semaphore_signal(barrier, inc=1, device_id=(me, up), device_id_type=MESH)

    neighbours = jnp.where(not_first, 1, 0) + jnp.where(not_last, 1, 0)
    pl.semaphore_wait(barrier, bits + neighbours)

    fwd = pltpu.make_async_remote_copy(outbuf, inbuf, fs, fr, device_id=(me, up), device_id_type=MESH)
    bwd = pltpu.make_async_remote_copy(gout, gin, bs, br, device_id=(me, down), device_id_type=MESH)

    mem_enc = inbuf.at[pl.ds(0, te)] if deep else enc
    mem_dec = inbuf.at[pl.ds(0, te)]
    stream = inbuf.at[pl.ds(te, td)] if deep else dec
    g_dec = gin.at[pl.ds(te, td)] if deep else cot
    g_enc = gin.at[pl.ds(0, te)]
    cols = 512

    if deep:

        @pl.when(p == 0)
        def _():
            inbuf[0:te, :] = enc[...]
            inbuf[te : te + td, :] = dec[...]

        @pl.when(p == layers - 1)
        def _():
            gin[0:te, :] = jnp.zeros((te, width), BF)
            gin[te : te + td, :] = cot[...]

    e_hot = one_hot(eid[...], te // micro_count, micro_count)

    def residual_out(src, row0, rows):
        for c in range(0, width, cols):
            y = dot(ab[0:rows, :], w_out[0, :, c : c + cols])
            outbuf[row0 : row0 + rows, c : c + cols] = (
                src[:, c : c + cols].astype(F32) + y
            ).astype(BF)

    def heads(q, k, v, rows, hot):
        qb[0:rows, :] = q
        kb[...] = k
        vb[...] = v
        allowed = t_dot(hot, e_hot) > 0.5
        prob = softmax_rows(dot_t(q, k) * scale, allowed)
        pb[0:rows, :] = prob
        ab[0:rows, :] = dot(prob.astype(BF), v).astype(BF)

    def heads_back(g, rows):
        prob = pb[0:rows, :]
        da = dot_t(g[...], w_out[0]).astype(BF)
        dv[...] = t_dot(prob.astype(BF), da).astype(BF)
        dp = dot_t(da, vb[...]).astype(BF).astype(F32)
        ds = prob * (dp - jnp.sum(prob * dp, axis=-1, keepdims=True)) * scale
        ds = ds.astype(BF)
        dq[0:rows, :] = dot(ds, kb[...]).astype(BF)
        dk[...] = t_dot(ds, qb[0:rows, :]).astype(BF)

    def rms_back(x_ref, pairs, r_ref, add, dst):
        for c in range(0, width, cols):
            dy = None
            for grad, which in pairs:
                term = dot_t(grad[0 : x_ref.shape[0], :], w_in[0, which, c : c + cols, :]).astype(BF)
                dy = term if dy is None else dy + term
            dst[:, c : c + cols] = dy

        step = 16

        def rows_back(i, carry):
            row = pl.ds(pl.multiple_of(i * step, step), step)
            dy = dst[row, :].astype(F32)
            x = x_ref[row, :].astype(F32)
            r = r_ref[row, :][:, 0:1]
            inner = jnp.mean(x * dy, axis=-1, keepdims=True)
            dx = (dy * r - x * (r * r * r * inner)).astype(BF)
            if add is not None:
                dx = dx + add[row, :]
            dst[row, :] = dx
            return carry

        lax.fori_loop(0, x_ref.shape[0] // step, rows_back, 0)

    def grads(left_q, left_kv, left_o, rows):
        for c in range(0, width, cols):
            lq = left_q[0:rows, c : c + cols]
            lkv = left_kv[:, c : c + cols]
            lo = left_o[:, c : c + cols]
            block = jnp.concatenate(
                [
                    t_dot(dq[0:rows, :], lq),
                    t_dot(dk[...], lkv),
                    t_dot(dv[...], lkv),
                    t_dot(ab[0:rows, :], lo),
                ],
                axis=0,
            ).astype(BF)
            size = width // n
            for j in range(cols // size):
                owner = c // size + j
                piece = block[:, j * size : (j + 1) * size]
                flip = [b[i] if not (owner >> i) & 1 else 1 - b[i] for i in range(bits)]
                for g, (lo_row, hi_row, order) in zip(gs, parts):
                    pos = sum(flip[s] * (1 << (bits - 1 - k)) for k, s in enumerate(order))
                    g[pos] = piece[lo_row:hi_row, :]

    @pl.when(not_first)
    def _():
        fwd.wait_recv()

    @pl.when(is_enc)
    def _():
        rms_rows(mem_enc, hbuf, rbuf if deep else None)
        h = hbuf[...]
        q, k, v = [dot(h, w_in[0, i]).astype(BF) for i in range(3)]
        heads(q, k, v, te, e_hot)
        residual_out(mem_enc, 0, te)
        if deep:
            outbuf[te : te + td, :] = inbuf[te : te + td, :]
        fwd.start()

    @pl.when(jnp.logical_not(is_enc))
    def _():
        rms_rows(stream, hbuf.at[pl.ds(0, td)], rsbuf if deep else None)
        rms_rows(mem_dec, mbuf, rbuf)
        q = dot(hbuf[0:td, :], w_in[0, 0]).astype(BF)
        m = mbuf[...]
        k = dot(m, w_in[0, 1]).astype(BF)
        v = dot(m, w_in[0, 2]).astype(BF)
        heads(q, k, v, td, one_hot(did[...], td // micro_count, micro_count))
        if deep:

            @pl.when(not_last)
            def _():
                outbuf[0:te, :] = inbuf[0:te, :]
                residual_out(stream, te, td)
                fwd.start()

    @pl.when(not_last)
    def _():
        bwd.wait_recv()

    @pl.when(jnp.logical_not(is_enc))
    def _():
        heads_back(g_dec, td)
        rms_back(mem_dec, ((dk, 1), (dv, 2)), rbuf, gin.at[pl.ds(0, te)] if deep else None,
                 gout.at[pl.ds(0, te)])
        if deep:
            rms_back(stream, ((dq, 0),), rsbuf, g_dec, gout.at[pl.ds(te, td)])
        bwd.start()
        grads(hbuf, mbuf, g_dec, td)

    @pl.when(is_enc)
    def _():
        heads_back(g_enc, te)
        if deep:

            @pl.when(not_first)
            def _():
                rms_back(mem_enc, ((dq, 0), (dk, 1), (dv, 2)), rbuf, g_enc,
                         gout.at[pl.ds(0, te)])
                gout[te : te + td, :] = gin[te : te + td, :]
                bwd.start()

        grads(hbuf, hbuf, g_enc, te)

    def stage(which, k):
        size = n >> (k + 1)
        return pltpu.make_async_remote_copy(
            gs[which].at[pl.ds(size, size)],
            recvs[which].at[pl.ds(size, size)],
            rs_send.at[which, k],
            rs_recv.at[which, k],
            device_id=(partner[parts[which][2][k]], p),
            device_id_type=MESH,
        )

    for which in range(count):
        stage(which, 0).start()
    for k in range(bits):
        size = n >> (k + 1)
        for which in range(count):
            stage(which, k).wait_recv()
            g, recv = gs[which], recvs[which]
            if k < bits - 1:

                def fold(j, carry):
                    g[j] = (g[j].astype(F32) + recv[size + j].astype(F32)).astype(BF)
                    return carry

                lax.fori_loop(0, size, fold, 0)
                stage(which, k + 1).start()
            else:
                lo_row, hi_row, _ = parts[which]
                total[lo_row:hi_row, :] = g[0].astype(F32) + recv[1].astype(F32)
    for i in range(3):
        out_in[0, i] = total[i * hd : (i + 1) * hd, :].T
    out_o[0] = total[3 * hd : 4 * hd, :]

    for which in range(count):
        for k in range(bits):
            stage(which, k).wait_send()

    @pl.when(not_last)
    def _():
        fwd.wait_send()

    @pl.when(not_first)
    def _():
        bwd.wait_send()


def body(enc_tokens, dec_tokens, enc_segments, dec_segments, proj_in, proj_out, cotangent):
    layers = lax.axis_size("pipe")
    n = lax.axis_size("dp")
    micro_count, te, width = enc_tokens.shape
    td = dec_tokens.shape[1]
    hd = proj_in.shape[3]
    te, td = te * micro_count, td * micro_count
    rows = te + (td if layers > 2 else 0)
    size = width // n
    bits = n.bit_length() - 1
    natural = tuple(range(bits))
    if bits == 4:
        parts = ((0, 192, (0, 1, 2, 3)), (192, 384, (1, 0, 2, 3)), (384, 512, (2, 3, 0, 1)))
    else:
        parts = ((0, 4 * hd, natural),)
    vm = pltpu.VMEM
    slots = [vm((n, hi - lo, size), BF) for lo, hi, _ in parts]
    dma = pltpu.SemaphoreType.DMA
    return pl.pallas_call(
        functools.partial(kernel, layers, n, micro_count, parts),
        out_shape=(
            jax.ShapeDtypeStruct((1, 3, size, hd), F32),
            jax.ShapeDtypeStruct((1, hd, size), F32),
        ),
        in_specs=[pl.BlockSpec(memory_space=pltpu.VMEM)] * 7,
        out_specs=(pl.BlockSpec(memory_space=pltpu.VMEM),) * 2,
        scratch_shapes=[
            vm((rows, width), BF),
            vm((rows, width), BF),
            vm((rows, width), BF),
            vm((rows, width), BF),
            vm((te, width), BF),
            vm((te, width), BF),
            vm((te, 128), F32),
            vm((td, 128), F32),
            vm((te, hd), BF),
            vm((te, hd), BF),
            vm((te, hd), BF),
            vm((te, hd), BF),
            vm((te, te), F32),
            vm((te, hd), BF),
            vm((te, hd), BF),
            vm((te, hd), BF),
            vm((4 * hd, size), F32),
            *slots,
            *slots,
            dma, dma, dma, dma,
            dma((len(parts), bits)),
            dma((len(parts), bits)),
        ],
        compiler_params=pltpu.CompilerParams(
            collective_id=0, has_side_effects=True, vmem_limit_bytes=56 << 20
        ),
    )(
        enc_tokens.reshape(te, width),
        dec_tokens.reshape(td, width),
        enc_segments.reshape(1, te),
        dec_segments.reshape(1, td),
        proj_in,
        proj_out,
        cotangent.reshape(td, width),
    )


def solution(mesh):
    return jax.shard_map(
        body,
        mesh=mesh,
        in_specs=(
            P(None, "dp", None),
            P(None, "dp", None),
            P(None, "dp"),
            P(None, "dp"),
            P("pipe", None, None, None),
            P("pipe", None, None),
            P(None, "dp", None),
        ),
        out_specs=(P("pipe", None, "dp", None), P("pipe", None, "dp")),
        check_vma=False,
    )
```

```python
import functools
import math

import jax
import jax.numpy as jnp
from jax import lax
from jax.experimental import pallas as pl
from jax.experimental.pallas import tpu as pltpu
from jax.sharding import PartitionSpec as P

BF = jnp.bfloat16
F32 = jnp.float32
MESH = pl.DeviceIdType.MESH
TN = (((1,), (1,)), ((), ()))
NT = (((0,), (0,)), ((), ()))


def dot(a, b):
    return jnp.dot(a, b, preferred_element_type=F32)


def dot_t(a, b):
    return lax.dot_general(a, b, TN, preferred_element_type=F32)


def t_dot(a, b):
    return lax.dot_general(a, b, NT, preferred_element_type=F32)


def one_hot(ids, per_micro, micro_count):
    rows = -(-(4 * micro_count) // 16) * 16
    count = ids.shape[1]
    which = lax.broadcasted_iota(jnp.int32, (rows, count), 0)
    micro = lax.broadcasted_iota(jnp.int32, (rows, count), 1) // per_micro
    return jnp.where(which == ids + 4 * micro, 1.0, 0.0).astype(BF)


def softmax_rows(scores, allowed):
    scores = jnp.where(allowed, scores, -1e30)
    expo = jnp.exp(scores - jnp.max(scores, axis=-1, keepdims=True))
    return expo / jnp.sum(expo, axis=-1, keepdims=True)


def rms_rows(src, dst, scale_ref, step=16):
    for row in range(0, src.shape[0], step):
        x = src[row : row + step, :].astype(F32)
        r = lax.rsqrt(jnp.mean(x * x, axis=-1, keepdims=True) + 1e-06)
        dst[row : row + step, :] = (x * r).astype(BF)
        if scale_ref is not None:
            scale_ref[row : row + step, :] = jnp.broadcast_to(r, (step, 128))


def kernel(
    layers, n, micro_count, parts,
    enc, dec, eid, did, w_in, w_out, cot,
    summed,
    inbuf, outbuf, gin, gout, hbuf, mbuf, rbuf, rsbuf, qb, kb, vb, ab, pb, dq, dk, dv, eids, dids, *rest,
):
    count = len(parts)
    gs = rest[:count]
    recvs = rest[count : 2 * count]
    fs, fr, bs, br, rs_send, rs_recv = rest[2 * count :]
    bits = n.bit_length() - 1
    half = layers // 2
    te, td = enc.shape[0], dec.shape[0]
    width = enc.shape[1]
    hd = w_in.shape[3]
    scale = 1.0 / math.sqrt(hd)
    deep = layers > 2

    p = lax.axis_index("pipe")
    me = lax.axis_index("dp")
    b = [lax.rem(me // (1 << i), 2) for i in range(bits)]
    partner = [me + (1 - 2 * b[i]) * (1 << i) for i in range(bits)]
    up = lax.rem(p + 1, layers)
    down = lax.rem(p + layers - 1, layers)
    not_first = p > 0
    not_last = p < layers - 1
    is_enc = p < half

    barrier = pltpu.get_barrier_semaphore()
    for q in partner:
        pl.semaphore_signal(barrier, inc=1, device_id=(q, p), device_id_type=MESH)

    @pl.when(not_first)
    def _():
        pl.semaphore_signal(barrier, inc=1, device_id=(me, down), device_id_type=MESH)

    @pl.when(not_last)
    def _():
        pl.semaphore_signal(barrier, inc=1, device_id=(me, up), device_id_type=MESH)

    neighbours = jnp.where(not_first, 1, 0) + jnp.where(not_last, 1, 0)
    pl.semaphore_wait(barrier, bits + neighbours)

    cols = 512
    chunks = width // cols
    cut = te // 2

    def fwd(i):
        part = (slice(None), pl.ds(i * cols, cols))
        return pltpu.make_async_remote_copy(
            outbuf.at[part], inbuf.at[part], fs.at[i], fr.at[i], device_id=(me, up), device_id_type=MESH
        )

    def bwd(i):
        part = pl.ds(0, cut) if i == 0 else pl.ds(cut, gout.shape[0] - cut)
        return pltpu.make_async_remote_copy(
            gout.at[part], gin.at[part], bs.at[i], br.at[i], device_id=(me, down), device_id_type=MESH
        )

    mem_enc = inbuf.at[pl.ds(0, te)] if deep else enc
    mem_dec = inbuf.at[pl.ds(0, te)]
    stream = inbuf.at[pl.ds(te, td)] if deep else dec
    g_dec = gin.at[pl.ds(te, td)] if deep else cot
    g_enc = gin.at[pl.ds(0, te)]

    if deep:

        @pl.when(p == 0)
        def _():
            inbuf[0:te, :] = enc[...]
            inbuf[te : te + td, :] = dec[...]

        @pl.when(p == layers - 1)
        def _():
            gin[0:te, :] = jnp.zeros((te, width), BF)
            gin[te : te + td, :] = cot[...]

    te1, td1 = te // micro_count, td // micro_count
    for i in range(micro_count):
        eids[:, i * te1 : (i + 1) * te1] = eid[i : i + 1, :]
        dids[:, i * td1 : (i + 1) * td1] = did[i : i + 1, :]
    e_hot = one_hot(eids[...], te1, micro_count)

    def residual_out(src, row0, rows):
        for c in range(0, width, cols):
            y = dot(ab[0:rows, :], w_out[0, :, c : c + cols])
            outbuf[row0 : row0 + rows, c : c + cols] = (
                src[:, c : c + cols].astype(F32) + y
            ).astype(BF)
            fwd(c // cols).start()

    def heads(q, k, v, rows, hot):
        qb[0:rows, :] = q
        kb[...] = k
        vb[...] = v
        allowed = t_dot(hot, e_hot) > 0.5
        prob = softmax_rows(dot_t(q, k) * scale, allowed)
        pb[0:rows, :] = prob
        ab[0:rows, :] = dot(prob.astype(BF), v).astype(BF)

    def heads_back(g, rows):
        prob = pb[0:rows, :]
        da = dot_t(g[...], w_out[0]).astype(BF)
        dv[...] = t_dot(prob.astype(BF), da).astype(BF)
        dp = dot_t(da, vb[...]).astype(BF).astype(F32)
        ds = prob * (dp - jnp.sum(prob * dp, axis=-1, keepdims=True)) * scale
        ds = ds.astype(BF)
        dq[0:rows, :] = dot(ds, kb[...]).astype(BF)
        dk[...] = t_dot(ds, qb[0:rows, :]).astype(BF)

    def rms_back(x_ref, pairs, r_ref, add, dst, early=True):
        for c in range(0, width, cols):
            dy = None
            for grad, which in pairs:
                term = dot_t(grad[0 : x_ref.shape[0], :], w_in[0, which, c : c + cols, :]).astype(BF)
                dy = term if dy is None else dy + term
            dst[:, c : c + cols] = dy

        step = 16

        def rows_back(i, carry):
            row = pl.ds(pl.multiple_of(i * step, step), step)
            dy = dst[row, :].astype(F32)
            x = x_ref[row, :].astype(F32)
            r = r_ref[row, :][:, 0:1]
            inner = jnp.mean(x * dy, axis=-1, keepdims=True)
            dx = (dy * r - x * (r * r * r * inner)).astype(BF)
            if add is not None:
                dx = dx + add[row, :]
            dst[row, :] = dx
            return carry

        steps = x_ref.shape[0] // step
        if early:
            lax.fori_loop(0, steps // 2, rows_back, 0)
            bwd(0).start()
            lax.fori_loop(steps // 2, steps, rows_back, 0)
        else:
            lax.fori_loop(0, steps, rows_back, 0)

    def stage(which, k):
        size = n >> (k + 1)
        return pltpu.make_async_remote_copy(
            gs[which].at[pl.ds(size, size)],
            recvs[which].at[pl.ds(size, size)],
            rs_send.at[which, k],
            rs_recv.at[which, k],
            device_id=(partner[parts[which][2][k]], p),
            device_id_type=MESH,
        )

    size = width // n

    def spread(block, c, base, chosen):
        for j in range(cols // size):
            owner = c // size + j
            piece = block[:, j * size : (j + 1) * size]
            flip = [b[i] if not (owner >> i) & 1 else 1 - b[i] for i in range(bits)]
            for which in chosen:
                lo_row, hi_row, order = parts[which]
                pos = sum(flip[s] * (1 << (bits - 1 - k)) for k, s in enumerate(order))
                gs[which][pos] = piece[lo_row - base : hi_row - base, :]

    out_parts = [i for i in range(count) if parts[i][0] >= 3 * hd]
    in_parts = [i for i in range(count) if parts[i][0] < 3 * hd]

    def out_grads(left_o, rows):
        for c in range(0, width, cols):
            block = t_dot(ab[0:rows, :], left_o[:, c : c + cols]).astype(BF)
            spread(block, c, 3 * hd, out_parts)
        for which in out_parts:
            stage(which, 0).start()

    def grads(left_q, left_kv, rows):
        for c in range(0, width, cols):
            lq = left_q[0:rows, c : c + cols]
            lkv = left_kv[:, c : c + cols]
            block = jnp.concatenate(
                [t_dot(dq[0:rows, :], lq), t_dot(dk[...], lkv), t_dot(dv[...], lkv)], axis=0
            ).astype(BF)
            spread(block, c, 0, in_parts)
        for which in in_parts:
            stage(which, 0).start()

    def decoder_query():
        rms_rows(stream, hbuf.at[pl.ds(0, td)], rsbuf if deep else None)
        qb[0:td, :] = dot(hbuf[0:td, :], w_in[0, 0]).astype(BF)

    if not deep:
        pl.when(jnp.logical_not(is_enc))(decoder_query)

    @pl.when(not_first)
    def _():
        for i in range(chunks):
            fwd(i).wait_recv()

    @pl.when(is_enc)
    def _():
        rms_rows(mem_enc, hbuf, rbuf if deep else None)
        h = hbuf[...]
        q, k, v = [dot(h, w_in[0, i]).astype(BF) for i in range(3)]
        heads(q, k, v, te, e_hot)
        if deep:
            outbuf[te : te + td, :] = inbuf[te : te + td, :]
        residual_out(mem_enc, 0, te)

    @pl.when(jnp.logical_not(is_enc))
    def _():
        if deep:
            decoder_query()
        rms_rows(mem_dec, mbuf, rbuf)
        q = qb[0:td, :]
        m = mbuf[...]
        k = dot(m, w_in[0, 1]).astype(BF)
        v = dot(m, w_in[0, 2]).astype(BF)
        heads(q, k, v, td, one_hot(dids[...], td1, micro_count))
        if deep:

            @pl.when(not_last)
            def _():
                outbuf[0:te, :] = inbuf[0:te, :]
                residual_out(stream, te, td)

    @pl.when(not_last)
    def _():
        for i in range(2):
            bwd(i).wait_recv()

    @pl.when(jnp.logical_not(is_enc))
    def _():
        heads_back(g_dec, td)
        rms_back(mem_dec, ((dk, 1), (dv, 2)), rbuf, gin.at[pl.ds(0, te)] if deep else None,
                 gout.at[pl.ds(0, te)])
        if deep:
            rms_back(stream, ((dq, 0),), rsbuf, g_dec, gout.at[pl.ds(te, td)], False)
        bwd(1).start()
        out_grads(g_dec, td)
        grads(hbuf, mbuf, td)

    @pl.when(is_enc)
    def _():
        out_grads(g_enc, te)
        heads_back(g_enc, te)
        if deep:

            @pl.when(not_first)
            def _():
                rms_back(mem_enc, ((dq, 0), (dk, 1), (dv, 2)), rbuf, g_enc,
                         gout.at[pl.ds(0, te)])
                gout[te : te + td, :] = gin[te : te + td, :]
                bwd(1).start()

        grads(hbuf, hbuf, te)

    for k in range(bits):
        size = n >> (k + 1)
        for which in range(count):
            stage(which, k).wait_recv()
            g, recv = gs[which], recvs[which]
            if k < bits - 1:

                def fold(j, carry):
                    g[j] = (g[j].astype(F32) + recv[size + j].astype(F32)).astype(BF)
                    return carry

                lax.fori_loop(0, size, fold, 0)
                stage(which, k + 1).start()
            else:
                lo_row, hi_row, _ = parts[which]
                summed[lo_row:hi_row, :] = g[0].astype(F32) + recv[1].astype(F32)
    for which in range(count):
        for k in range(bits):
            stage(which, k).wait_send()

    @pl.when(not_last)
    def _():
        for i in range(chunks):
            fwd(i).wait_send()

    @pl.when(not_first)
    def _():
        for i in range(2):
            bwd(i).wait_send()


def place(summed, out_in, out_o):
    hd = out_in.shape[3]
    for i in range(3):
        out_in[0, i] = summed[i * hd : (i + 1) * hd, :].T
    out_o[0] = summed[3 * hd : 4 * hd, :]


def body(enc_tokens, dec_tokens, enc_segments, dec_segments, proj_in, proj_out, cotangent):
    layers = lax.axis_size("pipe")
    n = lax.axis_size("dp")
    micro_count, te, width = enc_tokens.shape
    td = dec_tokens.shape[1]
    hd = proj_in.shape[3]
    te, td = te * micro_count, td * micro_count
    rows = te + (td if layers > 2 else 0)
    size = width // n
    bits = n.bit_length() - 1
    natural = tuple(range(bits))
    if bits == 4:
        xyz, yxz, zxy = (0, 1, 2, 3), (1, 0, 2, 3), (2, 3, 0, 1)
        parts = (
            (384, 448, zxy), (448, 512, zxy), (0, 96, xyz),
            (192, 288, yxz), (96, 192, xyz), (288, 384, yxz),
        )
    else:
        parts = ((3 * hd, 4 * hd, natural), (0, 3 * hd, natural))
    vm = pltpu.VMEM
    slots = [vm((n, hi - lo, size), BF) for lo, hi, _ in parts]
    dma = pltpu.SemaphoreType.DMA
    summed = pl.pallas_call(
        functools.partial(kernel, layers, n, micro_count, parts),
        out_shape=jax.ShapeDtypeStruct((4 * hd, size), F32),
        in_specs=[pl.BlockSpec(memory_space=pltpu.VMEM)] * 7,
        out_specs=pl.BlockSpec(memory_space=pltpu.VMEM),
        scratch_shapes=[
            vm((rows, width), BF),
            vm((rows, width), BF),
            vm((rows, width), BF),
            vm((rows, width), BF),
            vm((te, width), BF),
            vm((te, width), BF),
            vm((te, 128), F32),
            vm((td, 128), F32),
            vm((te, hd), BF),
            vm((te, hd), BF),
            vm((te, hd), BF),
            vm((te, hd), BF),
            vm((te, te), F32),
            vm((te, hd), BF),
            vm((te, hd), BF),
            vm((te, hd), BF),
            vm((1, te), jnp.int32),
            vm((1, td), jnp.int32),
            *slots,
            *slots,
            dma((width // 512,)), dma((width // 512,)), dma((2,)), dma((2,)),
            dma((len(parts), bits)),
            dma((len(parts), bits)),
        ],
        compiler_params=pltpu.CompilerParams(
            collective_id=0, has_side_effects=True, vmem_limit_bytes=56 << 20
        ),
    )(
        enc_tokens.reshape(te, width),
        dec_tokens.reshape(td, width),
        enc_segments,
        dec_segments,
        proj_in,
        proj_out,
        cotangent.reshape(td, width),
    )
    return pl.pallas_call(
        place,
        out_shape=(
            jax.ShapeDtypeStruct((1, 3, size, hd), F32),
            jax.ShapeDtypeStruct((1, hd, size), F32),
        ),
        in_specs=[pl.BlockSpec(memory_space=pltpu.VMEM)],
        out_specs=(pl.BlockSpec(memory_space=pltpu.VMEM),) * 2,
    )(summed)


def solution(mesh):
    return jax.shard_map(
        body,
        mesh=mesh,
        in_specs=(
            P(None, "dp", None),
            P(None, "dp", None),
            P(None, "dp"),
            P(None, "dp"),
            P("pipe", None, None, None),
            P("pipe", None, None),
            P(None, "dp", None),
        ),
        out_specs=(P("pipe", None, "dp", None), P("pipe", None, "dp")),
        check_vma=False,
    )
```

```python
import functools
import math

import jax
import jax.numpy as jnp
from jax import lax
from jax.experimental import pallas as pl
from jax.experimental.pallas import tpu as pltpu
from jax.sharding import PartitionSpec as P

BF = jnp.bfloat16
F32 = jnp.float32
MESH = pl.DeviceIdType.MESH
TN = (((1,), (1,)), ((), ()))
NT = (((0,), (0,)), ((), ()))


def dot(a, b):
    return jnp.dot(a, b, preferred_element_type=F32)


def dot_t(a, b):
    return lax.dot_general(a, b, TN, preferred_element_type=F32)


def t_dot(a, b):
    return lax.dot_general(a, b, NT, preferred_element_type=F32)


def one_hot(ids, per_micro, micro_count):
    rows = -(-(4 * micro_count) // 16) * 16
    count = ids.shape[1]
    which = lax.broadcasted_iota(jnp.int32, (rows, count), 0)
    micro = lax.broadcasted_iota(jnp.int32, (rows, count), 1) // per_micro
    return jnp.where(which == ids + 4 * micro, 1.0, 0.0).astype(BF)


def softmax_rows(scores, allowed):
    scores = jnp.where(allowed, scores, -1e30)
    expo = jnp.exp(scores - jnp.max(scores, axis=-1, keepdims=True))
    return expo / jnp.sum(expo, axis=-1, keepdims=True)


def rms_rows(src, dst, scale_ref, step=16):
    for row in range(0, src.shape[0], step):
        x = src[row : row + step, :].astype(F32)
        r = lax.rsqrt(jnp.mean(x * x, axis=-1, keepdims=True) + 1e-06)
        dst[row : row + step, :] = (x * r).astype(BF)
        if scale_ref is not None:
            scale_ref[row : row + step, :] = jnp.broadcast_to(r, (step, 128))


def kernel(
    layers, n, micro_count, parts,
    enc, dec, eid, did, w_in, w_out, cot,
    summed,
    inbuf, outbuf, gin, gout, hbuf, mbuf, rbuf, rsbuf, qb, kb, vb, ab, pb, dq, dk, dv, eids, dids, *rest,
):
    count = len(parts)
    gs = rest[:count]
    recvs = rest[count : 2 * count]
    fs, fr, bs, br, rs_send, rs_recv = rest[2 * count :]
    bits = n.bit_length() - 1
    half = layers // 2
    te, td = enc.shape[0], dec.shape[0]
    width = enc.shape[1]
    hd = w_in.shape[3]
    scale = 1.0 / math.sqrt(hd)
    deep = layers > 2

    p = lax.axis_index("pipe")
    me = lax.axis_index("dp")
    b = [lax.rem(me // (1 << i), 2) for i in range(bits)]
    partner = [me + (1 - 2 * b[i]) * (1 << i) for i in range(bits)]
    up = lax.rem(p + 1, layers)
    down = lax.rem(p + layers - 1, layers)
    not_first = p > 0
    not_last = p < layers - 1
    is_enc = p < half

    barrier = pltpu.get_barrier_semaphore()
    for q in partner:
        pl.semaphore_signal(barrier, inc=1, device_id=(q, p), device_id_type=MESH)

    @pl.when(not_first)
    def _():
        pl.semaphore_signal(barrier, inc=1, device_id=(me, down), device_id_type=MESH)

    @pl.when(not_last)
    def _():
        pl.semaphore_signal(barrier, inc=1, device_id=(me, up), device_id_type=MESH)

    cols = 512
    chunks = width // cols
    cut = te // 2

    def fwd(i):
        part = (slice(None), pl.ds(i * cols, cols))
        return pltpu.make_async_remote_copy(
            outbuf.at[part], inbuf.at[part], fs.at[i], fr.at[i], device_id=(me, up), device_id_type=MESH
        )

    def bwd(i):
        part = pl.ds(0, cut) if i == 0 else pl.ds(cut, gout.shape[0] - cut)
        return pltpu.make_async_remote_copy(
            gout.at[part], gin.at[part], bs.at[i], br.at[i], device_id=(me, down), device_id_type=MESH
        )

    mem_enc = inbuf.at[pl.ds(0, te)] if deep else enc
    mem_dec = inbuf.at[pl.ds(0, te)]
    stream = inbuf.at[pl.ds(te, td)] if deep else dec
    g_dec = gin.at[pl.ds(te, td)] if deep else cot
    g_enc = gin.at[pl.ds(0, te)]

    if deep:

        @pl.when(p == 0)
        def _():
            inbuf[0:te, :] = enc[...]
            inbuf[te : te + td, :] = dec[...]

        @pl.when(p == layers - 1)
        def _():
            gin[0:te, :] = jnp.zeros((te, width), BF)
            gin[te : te + td, :] = cot[...]

    te1, td1 = te // micro_count, td // micro_count
    for i in range(micro_count):
        eids[:, i * te1 : (i + 1) * te1] = eid[i : i + 1, :]
        dids[:, i * td1 : (i + 1) * td1] = did[i : i + 1, :]
    e_hot = one_hot(eids[...], te1, micro_count)

    def residual_out(src, row0, rows):
        for c in range(0, width, cols):
            y = dot(ab[0:rows, :], w_out[0, :, c : c + cols])
            outbuf[row0 : row0 + rows, c : c + cols] = (
                src[:, c : c + cols].astype(F32) + y
            ).astype(BF)
            fwd(c // cols).start()

    def heads(q, k, v, rows, hot):
        qb[0:rows, :] = q
        kb[...] = k
        vb[...] = v
        allowed = t_dot(hot, e_hot) > 0.5
        prob = softmax_rows(dot_t(q, k) * scale, allowed)
        pb[0:rows, :] = prob
        ab[0:rows, :] = dot(prob.astype(BF), v).astype(BF)

    def heads_back(g, rows):
        prob = pb[0:rows, :]
        da = dot_t(g[...], w_out[0]).astype(BF)
        dv[...] = t_dot(prob.astype(BF), da).astype(BF)
        dp = dot_t(da, vb[...]).astype(BF).astype(F32)
        ds = prob * (dp - jnp.sum(prob * dp, axis=-1, keepdims=True)) * scale
        ds = ds.astype(BF)
        dq[0:rows, :] = dot(ds, kb[...]).astype(BF)
        dk[...] = t_dot(ds, qb[0:rows, :]).astype(BF)

    def rms_back(x_ref, pairs, r_ref, add, dst, early=True):
        for c in range(0, width, cols):
            dy = None
            for grad, which in pairs:
                term = dot_t(grad[0 : x_ref.shape[0], :], w_in[0, which, c : c + cols, :]).astype(BF)
                dy = term if dy is None else dy + term
            dst[:, c : c + cols] = dy

        step = 16

        def rows_back(i, carry):
            row = pl.ds(pl.multiple_of(i * step, step), step)
            dy = dst[row, :].astype(F32)
            x = x_ref[row, :].astype(F32)
            r = r_ref[row, :][:, 0:1]
            inner = jnp.mean(x * dy, axis=-1, keepdims=True)
            dx = (dy * r - x * (r * r * r * inner)).astype(BF)
            if add is not None:
                dx = dx + add[row, :]
            dst[row, :] = dx
            return carry

        steps = x_ref.shape[0] // step
        if early:
            lax.fori_loop(0, steps // 2, rows_back, 0)
            bwd(0).start()
            lax.fori_loop(steps // 2, steps, rows_back, 0)
        else:
            lax.fori_loop(0, steps, rows_back, 0)

    def stage(which, k):
        size = n >> (k + 1)
        return pltpu.make_async_remote_copy(
            gs[which].at[pl.ds(size, size)],
            recvs[which].at[pl.ds(size, size)],
            rs_send.at[which, k],
            rs_recv.at[which, k],
            device_id=(partner[parts[which][2][k]], p),
            device_id_type=MESH,
        )

    size = width // n

    def spread(block, c, base, chosen):
        for j in range(cols // size):
            owner = c // size + j
            piece = block[:, j * size : (j + 1) * size]
            flip = [b[i] if not (owner >> i) & 1 else 1 - b[i] for i in range(bits)]
            for which in chosen:
                lo_row, hi_row, order = parts[which]
                pos = sum(flip[s] * (1 << (bits - 1 - k)) for k, s in enumerate(order))
                gs[which][pos] = piece[lo_row - base : hi_row - base, :]

    out_parts = [i for i in range(count) if parts[i][0] >= 3 * hd]
    in_parts = [i for i in range(count) if parts[i][0] < 3 * hd]

    def out_grads(left_o, rows):
        for c in range(0, width, cols):
            block = t_dot(ab[0:rows, :], left_o[:, c : c + cols]).astype(BF)
            spread(block, c, 3 * hd, out_parts)
        for which in out_parts:
            stage(which, 0).start()

    def grads(left_q, left_kv, rows):
        for c in range(0, width, cols):
            lq = left_q[0:rows, c : c + cols]
            lkv = left_kv[:, c : c + cols]
            block = jnp.concatenate(
                [t_dot(dq[0:rows, :], lq), t_dot(dk[...], lkv), t_dot(dv[...], lkv)], axis=0
            ).astype(BF)
            spread(block, c, 0, in_parts)
        for which in in_parts:
            stage(which, 0).start()

    def decoder_query():
        rms_rows(stream, hbuf.at[pl.ds(0, td)], rsbuf if deep else None)
        qb[0:td, :] = dot(hbuf[0:td, :], w_in[0, 0]).astype(BF)

    def encoder_heads():
        rms_rows(mem_enc, hbuf, rbuf if deep else None)
        h = hbuf[...]
        q, k, v = [dot(h, w_in[0, i]).astype(BF) for i in range(3)]
        heads(q, k, v, te, e_hot)

    if not deep:
        pl.when(jnp.logical_not(is_enc))(decoder_query)
        pl.when(is_enc)(encoder_heads)

    neighbours = jnp.where(not_first, 1, 0) + jnp.where(not_last, 1, 0)
    pl.semaphore_wait(barrier, bits + neighbours)

    @pl.when(not_first)
    def _():
        for i in range(chunks):
            fwd(i).wait_recv()

    @pl.when(is_enc)
    def _():
        if deep:
            encoder_heads()
            outbuf[te : te + td, :] = inbuf[te : te + td, :]
        residual_out(mem_enc, 0, te)

    @pl.when(jnp.logical_not(is_enc))
    def _():
        if deep:
            decoder_query()
        rms_rows(mem_dec, mbuf, rbuf)
        q = qb[0:td, :]
        m = mbuf[...]
        k = dot(m, w_in[0, 1]).astype(BF)
        v = dot(m, w_in[0, 2]).astype(BF)
        heads(q, k, v, td, one_hot(dids[...], td1, micro_count))
        if deep:

            @pl.when(not_last)
            def _():
                outbuf[0:te, :] = inbuf[0:te, :]
                residual_out(stream, te, td)

    @pl.when(not_last)
    def _():
        for i in range(2):
            bwd(i).wait_recv()

    @pl.when(jnp.logical_not(is_enc))
    def _():
        heads_back(g_dec, td)
        rms_back(mem_dec, ((dk, 1), (dv, 2)), rbuf, gin.at[pl.ds(0, te)] if deep else None,
                 gout.at[pl.ds(0, te)])
        if deep:
            rms_back(stream, ((dq, 0),), rsbuf, g_dec, gout.at[pl.ds(te, td)], False)
        bwd(1).start()
        out_grads(g_dec, td)
        grads(hbuf, mbuf, td)

    @pl.when(is_enc)
    def _():
        out_grads(g_enc, te)
        heads_back(g_enc, te)
        if deep:

            @pl.when(not_first)
            def _():
                rms_back(mem_enc, ((dq, 0), (dk, 1), (dv, 2)), rbuf, g_enc,
                         gout.at[pl.ds(0, te)])
                gout[te : te + td, :] = gin[te : te + td, :]
                bwd(1).start()

        grads(hbuf, hbuf, te)

    for k in range(bits):
        size = n >> (k + 1)
        for which in range(count):
            stage(which, k).wait_recv()
            g, recv = gs[which], recvs[which]
            if k < bits - 1:

                def fold(j, carry):
                    g[j] = (g[j].astype(F32) + recv[size + j].astype(F32)).astype(BF)
                    return carry

                lax.fori_loop(0, size, fold, 0)
                stage(which, k + 1).start()
            else:
                lo_row, hi_row, _ = parts[which]
                summed[lo_row:hi_row, :] = g[0].astype(F32) + recv[1].astype(F32)
    for which in range(count):
        for k in range(bits):
            stage(which, k).wait_send()

    @pl.when(not_last)
    def _():
        for i in range(chunks):
            fwd(i).wait_send()

    @pl.when(not_first)
    def _():
        for i in range(2):
            bwd(i).wait_send()


def place(summed, out_in, out_o):
    hd = out_in.shape[3]
    for i in range(3):
        out_in[0, i] = summed[i * hd : (i + 1) * hd, :].T
    out_o[0] = summed[3 * hd : 4 * hd, :]


def body(enc_tokens, dec_tokens, enc_segments, dec_segments, proj_in, proj_out, cotangent):
    layers = lax.axis_size("pipe")
    n = lax.axis_size("dp")
    micro_count, te, width = enc_tokens.shape
    td = dec_tokens.shape[1]
    hd = proj_in.shape[3]
    te, td = te * micro_count, td * micro_count
    rows = te + (td if layers > 2 else 0)
    size = width // n
    bits = n.bit_length() - 1
    natural = tuple(range(bits))
    if bits == 4:
        xyz, yxz, zxy = (0, 1, 2, 3), (1, 0, 2, 3), (2, 3, 0, 1)
        parts = (
            (384, 448, zxy), (448, 512, zxy), (0, 96, xyz),
            (192, 288, yxz), (96, 192, xyz), (288, 384, yxz),
        )
    else:
        parts = ((3 * hd, 4 * hd, natural), (0, 3 * hd, natural))
    vm = pltpu.VMEM
    slots = [vm((n, hi - lo, size), BF) for lo, hi, _ in parts]
    dma = pltpu.SemaphoreType.DMA
    summed = pl.pallas_call(
        functools.partial(kernel, layers, n, micro_count, parts),
        out_shape=jax.ShapeDtypeStruct((4 * hd, size), F32),
        in_specs=[pl.BlockSpec(memory_space=pltpu.VMEM)] * 7,
        out_specs=pl.BlockSpec(memory_space=pltpu.VMEM),
        scratch_shapes=[
            vm((rows, width), BF),
            vm((rows, width), BF),
            vm((rows, width), BF),
            vm((rows, width), BF),
            vm((te, width), BF),
            vm((te, width), BF),
            vm((te, 128), F32),
            vm((td, 128), F32),
            vm((te, hd), BF),
            vm((te, hd), BF),
            vm((te, hd), BF),
            vm((te, hd), BF),
            vm((te, te), F32),
            vm((te, hd), BF),
            vm((te, hd), BF),
            vm((te, hd), BF),
            vm((1, te), jnp.int32),
            vm((1, td), jnp.int32),
            *slots,
            *slots,
            dma((width // 512,)), dma((width // 512,)), dma((2,)), dma((2,)),
            dma((len(parts), bits)),
            dma((len(parts), bits)),
        ],
        compiler_params=pltpu.CompilerParams(
            collective_id=0, has_side_effects=True, vmem_limit_bytes=56 << 20
        ),
    )(
        enc_tokens.reshape(te, width),
        dec_tokens.reshape(td, width),
        enc_segments,
        dec_segments,
        proj_in,
        proj_out,
        cotangent.reshape(td, width),
    )
    return pl.pallas_call(
        place,
        out_shape=(
            jax.ShapeDtypeStruct((1, 3, size, hd), F32),
            jax.ShapeDtypeStruct((1, hd, size), F32),
        ),
        in_specs=[pl.BlockSpec(memory_space=pltpu.VMEM)],
        out_specs=(pl.BlockSpec(memory_space=pltpu.VMEM),) * 2,
    )(summed)


def solution(mesh):
    return jax.shard_map(
        body,
        mesh=mesh,
        in_specs=(
            P(None, "dp", None),
            P(None, "dp", None),
            P(None, "dp"),
            P(None, "dp"),
            P("pipe", None, None, None),
            P("pipe", None, None),
            P(None, "dp", None),
        ),
        out_specs=(P("pipe", None, "dp", None), P("pipe", None, "dp")),
        check_vma=False,
    )
```

```python
import functools
import math

import jax
import jax.numpy as jnp
from jax import lax
from jax.experimental import pallas as pl
from jax.experimental.pallas import tpu as pltpu
from jax.sharding import PartitionSpec as P

BF = jnp.bfloat16
F32 = jnp.float32
MESH = pl.DeviceIdType.MESH
TN = (((1,), (1,)), ((), ()))
NT = (((0,), (0,)), ((), ()))


def dot(a, b):
    return jnp.dot(a, b, preferred_element_type=F32)


def dot_t(a, b):
    return lax.dot_general(a, b, TN, preferred_element_type=F32)


def t_dot(a, b):
    return lax.dot_general(a, b, NT, preferred_element_type=F32)


def one_hot(ids, per_micro, micro_count):
    rows = -(-(4 * micro_count) // 16) * 16
    count = ids.shape[1]
    which = lax.broadcasted_iota(jnp.int32, (rows, count), 0)
    micro = lax.broadcasted_iota(jnp.int32, (rows, count), 1) // per_micro
    return jnp.where(which == ids + 4 * micro, 1.0, 0.0).astype(BF)


def softmax_rows(scores, allowed):
    scores = jnp.where(allowed, scores, -1e30)
    expo = jnp.exp(scores - jnp.max(scores, axis=-1, keepdims=True))
    return expo / jnp.sum(expo, axis=-1, keepdims=True)


def rms_rows(src, dst, scale_ref, step=16):
    for row in range(0, src.shape[0], step):
        x = src[row : row + step, :].astype(F32)
        r = lax.rsqrt(jnp.mean(x * x, axis=-1, keepdims=True) + 1e-06)
        dst[row : row + step, :] = (x * r).astype(BF)
        if scale_ref is not None:
            scale_ref[row : row + step, :] = jnp.broadcast_to(r, (step, 128))


def kernel(
    layers, n, micro_count, parts,
    enc, dec, eid, did, w_in, w_out, cot,
    summed,
    inbuf, outbuf, gin, gout, hbuf, mbuf, rbuf, rsbuf, qb, kb, vb, ab, pb, dq, dk, dv, eids, dids, w_got, a_got, *rest,
):
    count = len(parts)
    gs = rest[:count]
    recvs = rest[count : 2 * count]
    fs, fr, bs, br, rs_send, rs_recv = rest[2 * count :]
    bits = n.bit_length() - 1
    half = layers // 2
    te, td = enc.shape[0], dec.shape[0]
    width = enc.shape[1]
    hd = w_in.shape[3]
    scale = 1.0 / math.sqrt(hd)
    deep = layers > 2

    p = lax.axis_index("pipe")
    me = lax.axis_index("dp")
    b = [lax.rem(me // (1 << i), 2) for i in range(bits)]
    partner = [me + (1 - 2 * b[i]) * (1 << i) for i in range(bits)]
    up = lax.rem(p + 1, layers)
    down = lax.rem(p + layers - 1, layers)
    not_first = p > 0
    not_last = p < layers - 1
    is_enc = p < half

    barrier = pltpu.get_barrier_semaphore()
    for q in partner:
        pl.semaphore_signal(barrier, inc=1, device_id=(q, p), device_id_type=MESH)

    @pl.when(not_first)
    def _():
        pl.semaphore_signal(barrier, inc=1, device_id=(me, down), device_id_type=MESH)

    @pl.when(not_last)
    def _():
        pl.semaphore_signal(barrier, inc=1, device_id=(me, up), device_id_type=MESH)

    neighbours = jnp.where(not_first, 1, 0) + jnp.where(not_last, 1, 0)
    pl.semaphore_wait(barrier, bits + neighbours)

    cols = 512
    chunks = width // cols
    cut = te // 2

    def fwd(i):
        part = (slice(None), pl.ds(i * cols, cols))
        return pltpu.make_async_remote_copy(
            outbuf.at[part], inbuf.at[part], fs.at[i], fr.at[i], device_id=(me, up), device_id_type=MESH
        )

    def bwd(i):
        part = pl.ds(0, cut) if i == 0 else pl.ds(cut, gout.shape[0] - cut)
        return pltpu.make_async_remote_copy(
            gout.at[part], gin.at[part], bs.at[i], br.at[i], device_id=(me, down), device_id_type=MESH
        )

    def small(i):
        src, dst = ((w_out.at[0], w_got), (ab, a_got))[i]
        return pltpu.make_async_remote_copy(
            src, dst, fs.at[i], fr.at[i], device_id=(me, up), device_id_type=MESH
        )

    if not deep:

        @pl.when(is_enc)
        def _():
            small(0).start()

    mem_enc = inbuf.at[pl.ds(0, te)] if deep else enc
    mem_dec = inbuf.at[pl.ds(0, te)]
    stream = inbuf.at[pl.ds(te, td)] if deep else dec
    g_dec = gin.at[pl.ds(te, td)] if deep else cot
    g_enc = gin.at[pl.ds(0, te)]

    if deep:

        @pl.when(p == 0)
        def _():
            inbuf[0:te, :] = enc[...]
            inbuf[te : te + td, :] = dec[...]

        @pl.when(p == layers - 1)
        def _():
            gin[0:te, :] = jnp.zeros((te, width), BF)
            gin[te : te + td, :] = cot[...]

    te1, td1 = te // micro_count, td // micro_count
    for i in range(micro_count):
        eids[:, i * te1 : (i + 1) * te1] = eid[i : i + 1, :]
        dids[:, i * td1 : (i + 1) * td1] = did[i : i + 1, :]
    e_hot = one_hot(eids[...], te1, micro_count)

    def residual_out(src, row0, rows):
        for c in range(0, width, cols):
            y = dot(ab[0:rows, :], w_out[0, :, c : c + cols])
            outbuf[row0 : row0 + rows, c : c + cols] = (
                src[:, c : c + cols].astype(F32) + y
            ).astype(BF)
            fwd(c // cols).start()

    def heads(q, k, v, rows, hot):
        qb[0:rows, :] = q
        kb[...] = k
        vb[...] = v
        allowed = t_dot(hot, e_hot) > 0.5
        prob = softmax_rows(dot_t(q, k) * scale, allowed)
        pb[0:rows, :] = prob
        ab[0:rows, :] = dot(prob.astype(BF), v).astype(BF)

    def heads_back(g, rows):
        prob = pb[0:rows, :]
        da = dot_t(g[...], w_out[0]).astype(BF)
        dv[...] = t_dot(prob.astype(BF), da).astype(BF)
        dp = dot_t(da, vb[...]).astype(BF).astype(F32)
        ds = prob * (dp - jnp.sum(prob * dp, axis=-1, keepdims=True)) * scale
        ds = ds.astype(BF)
        dq[0:rows, :] = dot(ds, kb[...]).astype(BF)
        dk[...] = t_dot(ds, qb[0:rows, :]).astype(BF)

    def rms_back(x_ref, pairs, r_ref, add, dst, early=True):
        for c in range(0, width, cols):
            dy = None
            for grad, which in pairs:
                term = dot_t(grad[0 : x_ref.shape[0], :], w_in[0, which, c : c + cols, :]).astype(BF)
                dy = term if dy is None else dy + term
            dst[:, c : c + cols] = dy

        step = 16

        def rows_back(i, carry):
            row = pl.ds(pl.multiple_of(i * step, step), step)
            dy = dst[row, :].astype(F32)
            x = x_ref[row, :].astype(F32)
            r = r_ref[row, :][:, 0:1]
            inner = jnp.mean(x * dy, axis=-1, keepdims=True)
            dx = (dy * r - x * (r * r * r * inner)).astype(BF)
            if add is not None:
                dx = dx + add[row, :]
            dst[row, :] = dx
            return carry

        steps = x_ref.shape[0] // step
        if early:
            lax.fori_loop(0, steps // 2, rows_back, 0)
            bwd(0).start()
            lax.fori_loop(steps // 2, steps, rows_back, 0)
        else:
            lax.fori_loop(0, steps, rows_back, 0)

    def stage(which, k):
        size = n >> (k + 1)
        return pltpu.make_async_remote_copy(
            gs[which].at[pl.ds(size, size)],
            recvs[which].at[pl.ds(size, size)],
            rs_send.at[which, k],
            rs_recv.at[which, k],
            device_id=(partner[parts[which][2][k]], p),
            device_id_type=MESH,
        )

    size = width // n

    def spread(block, c, base, chosen):
        for j in range(cols // size):
            owner = c // size + j
            piece = block[:, j * size : (j + 1) * size]
            flip = [b[i] if not (owner >> i) & 1 else 1 - b[i] for i in range(bits)]
            for which in chosen:
                lo_row, hi_row, order = parts[which]
                pos = sum(flip[s] * (1 << (bits - 1 - k)) for k, s in enumerate(order))
                gs[which][pos] = piece[lo_row - base : hi_row - base, :]

    out_parts = [i for i in range(count) if parts[i][0] >= 3 * hd]
    in_parts = [i for i in range(count) if parts[i][0] < 3 * hd]

    def out_grads(left_o, rows):
        for c in range(0, width, cols):
            block = t_dot(ab[0:rows, :], left_o[:, c : c + cols]).astype(BF)
            spread(block, c, 3 * hd, out_parts)
        for which in out_parts:
            stage(which, 0).start()

    def grads(left_q, left_kv, rows):
        for c in range(0, width, cols):
            lq = left_q[0:rows, c : c + cols]
            lkv = left_kv[:, c : c + cols]
            block = jnp.concatenate(
                [t_dot(dq[0:rows, :], lq), t_dot(dk[...], lkv), t_dot(dv[...], lkv)], axis=0
            ).astype(BF)
            spread(block, c, 0, in_parts)
        for which in in_parts:
            stage(which, 0).start()

    def decoder_query():
        rms_rows(stream, hbuf.at[pl.ds(0, td)], rsbuf if deep else None)
        qb[0:td, :] = dot(hbuf[0:td, :], w_in[0, 0]).astype(BF)

    if not deep:
        pl.when(jnp.logical_not(is_enc))(decoder_query)

    @pl.when(not_first)
    def _():
        if deep:
            for i in range(chunks):
                fwd(i).wait_recv()
        else:
            small(0).wait_recv()
            small(1).wait_recv()
            for c in range(0, width, cols):
                y = dot(a_got[...], w_got[:, c : c + cols])
                inbuf[:, c : c + cols] = (enc[:, c : c + cols].astype(F32) + y).astype(BF)

    @pl.when(is_enc)
    def _():
        rms_rows(mem_enc, hbuf, rbuf if deep else None)
        h = hbuf[...]
        q, k, v = [dot(h, w_in[0, i]).astype(BF) for i in range(3)]
        heads(q, k, v, te, e_hot)
        if deep:
            outbuf[te : te + td, :] = inbuf[te : te + td, :]
            residual_out(mem_enc, 0, te)
        else:
            small(1).start()

    @pl.when(jnp.logical_not(is_enc))
    def _():
        if deep:
            decoder_query()
        rms_rows(mem_dec, mbuf, rbuf)
        q = qb[0:td, :]
        m = mbuf[...]
        k = dot(m, w_in[0, 1]).astype(BF)
        v = dot(m, w_in[0, 2]).astype(BF)
        heads(q, k, v, td, one_hot(dids[...], td1, micro_count))
        if deep:

            @pl.when(not_last)
            def _():
                outbuf[0:te, :] = inbuf[0:te, :]
                residual_out(stream, te, td)

    @pl.when(not_last)
    def _():
        for i in range(2):
            bwd(i).wait_recv()

    @pl.when(jnp.logical_not(is_enc))
    def _():
        heads_back(g_dec, td)
        rms_back(mem_dec, ((dk, 1), (dv, 2)), rbuf, gin.at[pl.ds(0, te)] if deep else None,
                 gout.at[pl.ds(0, te)])
        if deep:
            rms_back(stream, ((dq, 0),), rsbuf, g_dec, gout.at[pl.ds(te, td)], False)
        bwd(1).start()
        out_grads(g_dec, td)
        grads(hbuf, mbuf, td)

    @pl.when(is_enc)
    def _():
        out_grads(g_enc, te)
        heads_back(g_enc, te)
        if deep:

            @pl.when(not_first)
            def _():
                rms_back(mem_enc, ((dq, 0), (dk, 1), (dv, 2)), rbuf, g_enc,
                         gout.at[pl.ds(0, te)])
                gout[te : te + td, :] = gin[te : te + td, :]
                bwd(1).start()

        grads(hbuf, hbuf, te)

    for k in range(bits):
        size = n >> (k + 1)
        for which in range(count):
            stage(which, k).wait_recv()
            g, recv = gs[which], recvs[which]
            if k < bits - 1:

                def fold(j, carry):
                    g[j] = (g[j].astype(F32) + recv[size + j].astype(F32)).astype(BF)
                    return carry

                lax.fori_loop(0, size, fold, 0)
                stage(which, k + 1).start()
            else:
                lo_row, hi_row, _ = parts[which]
                summed[lo_row:hi_row, :] = g[0].astype(F32) + recv[1].astype(F32)
    for which in range(count):
        for k in range(bits):
            stage(which, k).wait_send()

    @pl.when(not_last)
    def _():
        if deep:
            for i in range(chunks):
                fwd(i).wait_send()
        else:
            small(0).wait_send()
            small(1).wait_send()

    @pl.when(not_first)
    def _():
        for i in range(2):
            bwd(i).wait_send()


def place(summed, out_in, out_o):
    hd = out_in.shape[3]
    for i in range(3):
        out_in[0, i] = summed[i * hd : (i + 1) * hd, :].T
    out_o[0] = summed[3 * hd : 4 * hd, :]


def body(enc_tokens, dec_tokens, enc_segments, dec_segments, proj_in, proj_out, cotangent):
    layers = lax.axis_size("pipe")
    n = lax.axis_size("dp")
    micro_count, te, width = enc_tokens.shape
    td = dec_tokens.shape[1]
    hd = proj_in.shape[3]
    te, td = te * micro_count, td * micro_count
    rows = te + (td if layers > 2 else 0)
    size = width // n
    bits = n.bit_length() - 1
    natural = tuple(range(bits))
    if bits == 4:
        xyz, yxz, zxy = (0, 1, 2, 3), (1, 0, 2, 3), (2, 3, 0, 1)
        parts = (
            (384, 448, zxy), (448, 512, zxy), (0, 96, xyz),
            (192, 288, yxz), (96, 192, xyz), (288, 384, yxz),
        )
    else:
        parts = ((3 * hd, 4 * hd, natural), (0, 3 * hd, natural))
    vm = pltpu.VMEM
    slots = [vm((n, hi - lo, size), BF) for lo, hi, _ in parts]
    dma = pltpu.SemaphoreType.DMA
    summed = pl.pallas_call(
        functools.partial(kernel, layers, n, micro_count, parts),
        out_shape=jax.ShapeDtypeStruct((4 * hd, size), F32),
        in_specs=[pl.BlockSpec(memory_space=pltpu.VMEM)] * 7,
        out_specs=pl.BlockSpec(memory_space=pltpu.VMEM),
        scratch_shapes=[
            vm((rows, width), BF),
            vm((rows, width), BF),
            vm((rows, width), BF),
            vm((rows, width), BF),
            vm((te, width), BF),
            vm((te, width), BF),
            vm((te, 128), F32),
            vm((td, 128), F32),
            vm((te, hd), BF),
            vm((te, hd), BF),
            vm((te, hd), BF),
            vm((te, hd), BF),
            vm((te, te), F32),
            vm((te, hd), BF),
            vm((te, hd), BF),
            vm((te, hd), BF),
            vm((1, te), jnp.int32),
            vm((1, td), jnp.int32),
            vm((hd, width), BF),
            vm((te, hd), BF),
            *slots,
            *slots,
            dma((width // 512,)), dma((width // 512,)), dma((2,)), dma((2,)),
            dma((len(parts), bits)),
            dma((len(parts), bits)),
        ],
        compiler_params=pltpu.CompilerParams(
            collective_id=0, has_side_effects=True, vmem_limit_bytes=56 << 20
        ),
    )(
        enc_tokens.reshape(te, width),
        dec_tokens.reshape(td, width),
        enc_segments,
        dec_segments,
        proj_in,
        proj_out,
        cotangent.reshape(td, width),
    )
    return pl.pallas_call(
        place,
        out_shape=(
            jax.ShapeDtypeStruct((1, 3, size, hd), F32),
            jax.ShapeDtypeStruct((1, hd, size), F32),
        ),
        in_specs=[pl.BlockSpec(memory_space=pltpu.VMEM)],
        out_specs=(pl.BlockSpec(memory_space=pltpu.VMEM),) * 2,
    )(summed)


def solution(mesh):
    return jax.shard_map(
        body,
        mesh=mesh,
        in_specs=(
            P(None, "dp", None),
            P(None, "dp", None),
            P(None, "dp"),
            P(None, "dp"),
            P("pipe", None, None, None),
            P("pipe", None, None),
            P(None, "dp", None),
        ),
        out_specs=(P("pipe", None, "dp", None), P("pipe", None, "dp")),
        check_vma=False,
    )
```
